32 devices in a mesh: blk: 8 (over z, y), head: 4 (over x, core).
Axes of the slice: x: 2, y: 2, z: 4, core: 2. Of those that a mesh axis runs over, the one named last changes fastest.
Arguments:
- query_heads: bfloat16 [1536, 24576], P('blk', 'head'), may hold values from -200 to 200
- latent_cache: bfloat16 [1536, 512], P('blk'), may hold values from -6 to 6
- rope_keys: bfloat16 [1536, 64], P('blk'), may hold values from -10 to 10
- up_weight: bfloat16 [512, 32768], P('blk', 'head'), may hold values from -0.25 to 0.25
- out_weight: bfloat16 [16384, 5120], P('head'), may hold values from -0.046875 to 0.046875
- block_mask: int32 [16, 16], replicated, may hold values from 0 to 1, as said below
Outputs:
- attended: bfloat16 [1536, 5120], P('blk', 'head')
The draws below stay inside these ranges and needn't reach their ends.
Inputs may be any that keep to these rules, and one draw needn't show every extreme that they name: block_mask[i, i] is 1 and block_mask[i, j] is 0 for j > i; entries below the diagonal are 0 or 1.
All inputs are finite; a program needn't handle non-finite values.
Results may differ from the reference program's by a relative error of at most 0.019.
Values may be sent and summed in bfloat16 or wider, within the bound.
A program may use at most 128 MiB of HBM per device.

```python
import math
import jax
import jax.numpy as jnp
from jax import lax

D = 5120
H = 128
DN = 128
DR = 64
DV = 128
KVR = 512
QB = 96
TOKENS = 1536
NBLK = 16
N_HEAD = 4


def draw_query_heads(key, part):
    shape = (TOKENS, H, DN + DR)
    base_draw = jnp.clip(jax.random.normal(jax.random.fold_in(key, 1), shape, jnp.float32), -6.0, 6.0)
    return base_draw.reshape(TOKENS, H * (DN + DR)).astype(jnp.bfloat16)


def draw_rope_keys(key, part):
    shape = (TOKENS, DR)
    base_draw = jnp.clip(jax.random.normal(jax.random.fold_in(key, 2), shape, jnp.float32), -6.0, 6.0)
    return base_draw.astype(jnp.bfloat16)


def draw_block_mask(key, part):
    random_bits = jax.random.randint(jax.random.fold_in(key, 3), (NBLK, NBLK), 0, 2)
    row_index = jnp.arange(NBLK)[:, None]
    column_index = jnp.arange(NBLK)[None, :]
    kept = jnp.where(column_index == row_index, 1, jnp.where(column_index < row_index, random_bits, 0))
    return kept.astype(jnp.int32)


def level_of(rng, shape, cuts, least, top_value):
    def one(axis_at, shards_of):
        steps = jax.random.uniform(jax.random.fold_in(jax.random.fold_in(rng, 6), axis_at), (shards_of,), jnp.float32, least / len(cuts), top_value / len(cuts))
        return jnp.repeat(jnp.exp(steps), shape[axis_at] // shards_of).reshape((-1,) + (1,) * (len(shape) - axis_at - 1))

    level = one(*cuts[0])
    for cut in cuts[1:]:
        level = level * one(*cut)
    return level


def bell_draw(own_key, shape, spread, reach, pieces=(), kind=jnp.bfloat16):
    loudness = level_of(own_key, shape, pieces, -0.22, 0.18) if pieces else 1.0
    values = jax.random.normal(own_key, shape, jnp.float32) * spread * loudness
    return jnp.minimum(jnp.maximum(values, -reach), reach).astype(kind)


def setup_inputs(seed: int = 0) -> dict:
    arg_keys = jax.random.split(jax.random.key(seed), 7)
    return {
        "query_heads": draw_query_heads(jax.random.fold_in(arg_keys[6], 71), 0),
        "latent_cache": bell_draw(arg_keys[1], (TOKENS, KVR), 1.0, 6.0, ((0, 8),)),
        "rope_keys": draw_rope_keys(jax.random.fold_in(arg_keys[6], 71), 0),
        "up_weight": bell_draw(arg_keys[3], (KVR, H * (DN + DV)), KVR ** -0.5, 0.25, ((0, 8), (1, 4))),
        "out_weight": bell_draw(arg_keys[4], (H * DV, D), (H * DV) ** -0.5, 0.046875, ((0, 4),)),
        "block_mask": draw_block_mask(jax.random.fold_in(arg_keys[6], 71), 0),
    }


NEG_FILL = -1e+30

def reference(query_heads, latent_cache, rope_keys, up_weight, out_weight, block_mask):
    token_count = query_heads.shape[0]
    queries = query_heads.reshape(token_count, H, DN + DR)
    expanded = jnp.dot(latent_cache, up_weight, preferred_element_type=jnp.float32).astype(jnp.bfloat16)
    expanded = expanded.reshape(token_count, H, DN + DV)
    position = jnp.arange(token_count, dtype=jnp.int32)
    block_id = position // QB
    block_rows = jnp.take(block_mask, block_id, axis=0)
    block_bits = jnp.take(block_rows, block_id, axis=1)
    allowed = (block_bits == 1) & (position[None, :] <= position[:, None])
    score_scale = 1.0 / math.sqrt(DN + DR)

    def one_head(operands):
        query_part, key_value = operands
        scores = jnp.dot(query_part[:, :DN], key_value[:, :DN].T, preferred_element_type=jnp.float32)
        scores = scores + jnp.dot(query_part[:, DN:], rope_keys.T, preferred_element_type=jnp.float32)
        scores = jnp.where(allowed, scores * score_scale, NEG_FILL)
        row_max = lax.optimization_barrier(jnp.max(scores, axis=1, keepdims=True))
        weights = jnp.where(allowed, jnp.exp(scores - row_max), 0.0)
        denominator = lax.optimization_barrier(jnp.sum(weights, axis=1, keepdims=True))
        mixed = jnp.dot(weights.astype(jnp.bfloat16), key_value[:, DN:], preferred_element_type=jnp.float32)
        return (mixed / denominator).astype(jnp.bfloat16)
    per_head = lax.map(one_head, (jnp.transpose(queries, (1, 0, 2)), jnp.transpose(expanded, (1, 0, 2))))
    group_width = H // N_HEAD * DV
    outputs = jnp.transpose(per_head, (1, 0, 2)).reshape(token_count, N_HEAD, group_width)
    outputs = jnp.transpose(outputs, (1, 0, 2))
    weight_groups = out_weight.reshape(N_HEAD, group_width, D)

    def add_group(running_sum, operands):
        partial_sum = jnp.dot(operands[0], operands[1], preferred_element_type=jnp.float32).astype(jnp.bfloat16)
        partial_sum = lax.optimization_barrier(partial_sum)
        return (running_sum + partial_sum.astype(jnp.float32), None)
    summed_out, unused = lax.scan(add_group, jnp.zeros((token_count, D), jnp.float32), (outputs, weight_groups))
    return summed_out.astype(jnp.bfloat16)
```

```python
import functools
import math

import jax
import jax.numpy as jnp
from jax import lax
from jax.experimental import pallas as pl
from jax.experimental.pallas import tpu as pltpu
from jax.sharding import PartitionSpec as P

DN = 128
DR = 64
DV = 128
QB = 96
NEG = -1e30
HPC = 4
PARTS = 4
MESH = pl.DeviceIdType.MESH


def ring_place(index, n):
    return jnp.where(index % 2 == 0, index // 2, n - 1 - index // 2)


def ring_index(place, n):
    place = lax.rem(place + 2 * n, n)
    return jnp.where(place < n // 2, 2 * place, 2 * (n - 1 - place) + 1)


def kernel(
    n, nh, mask_ref, q_ref, lat_ref, up_ref, ow_ref, out_ref,
    wfull, lat, wo, acc, scores, peak, qs, vals, mix, bias, heads_out,
    give1, take1, give2, take2,
    cw_send, cw_recv, cc_send, cc_recv,
    lcw_send, lcw_recv, lcc_send, lcc_recv, lp_send, lp_recv,
    wo_sem, r1_send, r1_recv, r2_send, r2_recv,
):
    tok = q_ref.shape[0]
    rows = up_ref.shape[0]
    nchunk, _, cw = wfull.shape
    half = n // 2
    kc = 2 * tok
    kvr = n * rows
    ocols = out_ref.shape[1]
    nchip = nh // 2
    my = lax.axis_index("blk")
    hd = lax.axis_index("head")
    place = ring_place(my, n)
    right = ring_index(place + 1, n)
    left = ring_index(place + n - 1, n)
    part = lax.rem(hd, PARTS)
    base = hd - part
    prow = tok // PARTS
    core = lax.rem(hd, 2)
    chip = hd // 2
    mate = chip * 2 + 1 - core
    scale = math.log2(math.e) / math.sqrt(DN + DR)

    barrier = pltpu.get_barrier_semaphore()
    for other in (left, right):
        pl.semaphore_signal(barrier, inc=1, device_id=(other, hd), device_id_type=MESH)
    for d in range(1, nh):
        pl.semaphore_signal(barrier, inc=1, device_id=(my, lax.rem(hd + d, nh)), device_id_type=MESH)
    pl.semaphore_wait(barrier, 2 + nh - 1)

    def wmsg(c, k, clockwise):
        origin = ring_index(place - (k - 1), n) if clockwise else ring_index(place + (k - 1), n)
        start, size = origin * rows, rows
        if k == half:
            size = rows // 2
            if not clockwise:
                start = start + size
        block = wfull.at[c, pl.ds(pl.multiple_of(start, 16), size), :]
        return pltpu.make_async_remote_copy(
            src_ref=block, dst_ref=block,
            send_sem=(cw_send if clockwise else cc_send).at[c, k - 1],
            recv_sem=(cw_recv if clockwise else cc_recv).at[c, k - 1],
            device_id=(right if clockwise else left, hd), device_id_type=MESH,
        )

    def wgot(c, k, clockwise):
        origin = ring_index(place - k, n) if clockwise else ring_index(place + k, n)
        start, size = origin * rows, rows
        if k == half:
            size = rows // 2
            if not clockwise:
                start = start + size
        block = wfull.at[c, pl.ds(pl.multiple_of(start, 16), size), :]
        return pltpu.make_async_remote_copy(
            src_ref=block, dst_ref=block,
            send_sem=(cw_send if clockwise else cc_send).at[c, k - 1],
            recv_sem=(cw_recv if clockwise else cc_recv).at[c, k - 1],
            device_id=(right if clockwise else left, hd), device_id_type=MESH,
        )

    def lmsg(k, clockwise, received):
        steps = k if received else k - 1
        origin = ring_index(place - steps, n) if clockwise else ring_index(place + steps, n)
        block = lat.at[origin, part]
        return pltpu.make_async_remote_copy(
            src_ref=block, dst_ref=block,
            send_sem=(lcw_send if clockwise else lcc_send).at[k - 1],
            recv_sem=(lcw_recv if clockwise else lcc_recv).at[k - 1],
            device_id=(right if clockwise else left, hd), device_id_type=MESH,
        )

    def lpeer(k, clockwise, d, received):
        origin = ring_index(place - k, n) if clockwise else ring_index(place + k, n)
        e = (k - 1) * 2 + (0 if clockwise else 1)
        owner = lax.rem(part + PARTS - d, PARTS) if received else part
        block = lat.at[origin, owner]
        return pltpu.make_async_remote_copy(
            src_ref=block, dst_ref=block,
            send_sem=lp_send.at[e, d - 1], recv_sem=lp_recv.at[e, d - 1],
            device_id=(my, base + lax.rem(part + d, PARTS)), device_id_type=MESH,
        )

    lat_hops = [(k, way) for k in range(1, half + 1) for way in (True, False) if way or k < half]

    lat[my] = lat_ref[...].reshape(PARTS, prow, lat_ref.shape[1])
    lmsg(1, True, False).start()
    lmsg(1, False, False).start()

    own_rows = pl.ds(pl.multiple_of(my * rows, 16), rows)

    def fill(c, _):
        wfull[c, own_rows, :] = up_ref[:, pl.ds(pl.multiple_of(c * cw, 128), cw)]
        return 0

    lax.fori_loop(0, nchunk, fill, 0)

    def wo_copy(c):
        slot = lax.rem(c, 2)
        return pltpu.make_async_copy(
            ow_ref.at[pl.ds(pl.multiple_of(c * (HPC * DV), 128), HPC * DV), :],
            wo.at[slot], wo_sem.at[slot],
        )

    nj = my // 2 + 1

    def send_group(t, k):
        c = t - (k - 1)

        @pl.when((c >= 0) & (c < nchunk))
        def _():
            if k > 1:
                wgot(c, k - 1, True).wait_recv()
            wmsg(c, k, True).start()
            if k > 1:
                wgot(c, k - 1, False).wait_recv()
            wmsg(c, k, False).start()

    def project(c, o):
        slot = lax.rem(c, 2)
        columns = pl.ds(pl.multiple_of(o * ocols, 128), ocols)
        return acc[o] + jnp.dot(
            heads_out[...], wo[slot, :, columns], preferred_element_type=jnp.float32
        )

    def phase_a(c):
        qc = q_ref[:, pl.ds(pl.multiple_of(c * (HPC * (DN + DR)), 128), HPC * (DN + DR))]
        pad = jnp.zeros((tok, 256 - DN - DR), qc.dtype)
        for h in range(HPC):
            qs[h] = jnp.concatenate([qc[:, h * (DN + DR) : (h + 1) * (DN + DR)], pad], axis=1)
            peak[h] = jnp.full((tok, 128), NEG, jnp.float32)
            mix[h] = jnp.zeros((tok, 256), jnp.float32)

        def step(j, _):
            block = lat[pl.ds(2 * j, 2)].reshape(kc, lat_ref.shape[1])
            rope = block[:, kvr:]
            kv = jnp.dot(
                block[:, :kvr], wfull[c], preferred_element_type=jnp.float32
            ).astype(jnp.bfloat16)
            for h in range(HPC):
                key = jnp.concatenate([kv[:, h * 256 : h * 256 + DN], rope], axis=1)
                vals[h, j] = kv[:, h * 256 + DN : (h + 1) * 256]
                s = lax.dot_general(
                    qs[h], key, (((1,), (1,)), ((), ())), preferred_element_type=jnp.float32
                )
                s = s * scale + bias[j]
                scores[h, j] = s
                top = peak[h]
                for g in range(kc // 128):
                    top = jnp.maximum(top, s[:, g * 128 : (g + 1) * 128])
                peak[h] = top
            return 0

        lax.fori_loop(0, nj, step, 0)

    def phase_b():
        for h in range(HPC):
            peak[h] = jnp.broadcast_to(jnp.max(peak[h], axis=1, keepdims=True), (tok, 128))
        ones = jnp.ones((kc, 128), jnp.bfloat16)

        def step(j, _):
            for h in range(HPC):
                top = peak[h]
                p = jnp.concatenate(
                    [
                        jnp.exp2(scores[h, j, :, g * 128 : (g + 1) * 128] - top).astype(jnp.bfloat16)
                        for g in range(kc // 128)
                    ],
                    axis=1,
                )
                v = jnp.concatenate([vals[h, j], ones], axis=1)
                mix[h] += jnp.dot(p, v, preferred_element_type=jnp.float32)
            return 0

        lax.fori_loop(0, nj, step, 0)
        for h in range(HPC):
            m = mix[h]
            heads_out[:, h * DV : (h + 1) * DV] = (m[:, :DV] / m[:, DV:]).astype(jnp.bfloat16)

    def tick(t, _):
        c = t - half
        live = c >= 0
        upper = list(range(half, 0, -1))
        first = upper[: max(1, half // 2)]
        second = upper[max(1, half // 2) :]
        for k in first:
            send_group(t, k)

        for k, way in lat_hops:
            @pl.when(t == k)
            def _(k=k, way=way):
                lmsg(k, way, True).wait_recv()
                if (k + 1, way) in lat_hops:
                    lmsg(k + 1, way, False).start()
                for d in range(1, PARTS):
                    lpeer(k, way, d, False).start()

        @pl.when(t == 0)
        def _():
            wo_copy(0).start()
            wo_copy(1).start()
            acc[...] = jnp.zeros_like(acc)
            lane = lax.broadcasted_iota(jnp.int32, (QB, kc), 1)
            row = lax.broadcasted_iota(jnp.int32, (QB, kc), 0)
            group = lane // QB
            for j in range(n // 2):
                for g in range(tok // QB):
                    bits = jnp.zeros((QB, kc), jnp.int32)
                    for b in range(kc // QB):
                        bit = mask_ref[my * (tok // QB) + g, j * (kc // QB) + b]
                        bits = jnp.where(group == b, bit, bits)
                    allowed = (bits == 1) & (lane + j * kc <= row + (my * tok + g * QB))
                    bias[j, g * QB : (g + 1) * QB, :] = jnp.where(allowed, 0.0, NEG)

        @pl.when(t == half)
        def _():
            for k, way in lat_hops:
                for d in range(1, PARTS):
                    lpeer(k, way, d, True).wait_recv()

        @pl.when(live)
        def _():
            wgot(c, half, True).wait_recv()
            wgot(c, half, False).wait_recv()
            phase_a(c)

        for k in second:
            send_group(t, k)

        @pl.when(live)
        def _():
            phase_b()
            wo_copy(c).wait()

        @pl.when(live & (c < nchunk - 1))
        def _():
            def one(o, _):
                acc[o] = project(c, o)
                return 0

            lax.fori_loop(0, nh, one, 0)

            @pl.when(c + 2 < nchunk)
            def _():
                wo_copy(c + 2).start()

        return 0

    lax.fori_loop(0, nchunk + half, tick, 0)

    last = nchunk - 1

    def stage1(i):
        return pltpu.make_async_remote_copy(
            src_ref=give1.at[i], dst_ref=take1.at[i], send_sem=r1_send.at[i],
            recv_sem=r1_recv.at[i], device_id=(my, mate), device_id_type=MESH,
        )

    def stage2(i):
        to = lax.rem(chip + i, nchip) * 2 + core
        return pltpu.make_async_remote_copy(
            src_ref=give2.at[i - 1], dst_ref=take2.at[i - 1], send_sem=r2_send.at[i - 1],
            recv_sem=r2_recv.at[i - 1], device_id=(my, to), device_id_type=MESH,
        )

    order = list(range(1, nchip)) + [0]
    for i in order:
        to = lax.rem(chip + i, nchip) * 2 + 1 - core
        give1[i] = project(last, to).astype(jnp.bfloat16)
        stage1(i).start()
    for i in order[:-1]:
        to = lax.rem(chip + i, nchip) * 2 + core
        mine = project(last, to)
        stage1(i).wait_recv()
        give2[i - 1] = (mine + take1[i].astype(jnp.float32)).astype(jnp.bfloat16)
        stage2(i).start()
    total = project(last, hd)
    stage1(0).wait_recv()
    total = total + take1[0].astype(jnp.float32)
    acc[0] = total
    for i in order[:-1]:
        stage2(i).wait_recv()
        acc[0] += take2[i - 1].astype(jnp.float32)
    out_ref[...] = acc[0].astype(jnp.bfloat16)

    def drain(c, _):
        for k in range(1, half + 1):
            wmsg(c, k, True).wait_send()
            wmsg(c, k, False).wait_send()
        return 0

    lax.fori_loop(0, nchunk, drain, 0)
    for k, way in lat_hops:
        lmsg(k, way, False).wait_send()
        for d in range(1, PARTS):
            lpeer(k, way, d, False).wait_send()
    for i in order:
        stage1(i).wait_send()
    for i in order[:-1]:
        stage2(i).wait_send()


def per_device(n, nh, query_heads, latent_cache, rope_keys, up_weight, out_weight, block_mask):
    tok = query_heads.shape[0]
    heads = out_weight.shape[0] // DV
    kvr = latent_cache.shape[1]
    rows = up_weight.shape[0]
    width = out_weight.shape[1]
    ocols = width // nh
    nchunk = heads // HPC
    half = n // 2
    kc = 2 * tok
    lw = kvr + 128
    latent = jnp.concatenate(
        [latent_cache, rope_keys, jnp.zeros((tok, 128 - DR), latent_cache.dtype)], axis=1
    )
    bf16, f32 = jnp.bfloat16, jnp.float32
    dma = pltpu.SemaphoreType.DMA
    nchip = nh // 2
    vmem = pl.BlockSpec(memory_space=pltpu.VMEM)
    return pl.pallas_call(
        functools.partial(kernel, n, nh),
        out_shape=jax.ShapeDtypeStruct((tok, ocols), bf16),
        in_specs=[
            pl.BlockSpec(memory_space=pltpu.SMEM), vmem, vmem, vmem,
            pl.BlockSpec(memory_space=pl.ANY),
        ],
        out_specs=vmem,
        scratch_shapes=[
            pltpu.VMEM((nchunk, kvr, HPC * 256), bf16),
            pltpu.VMEM((n, PARTS, tok // PARTS, lw), bf16),
            pltpu.VMEM((2, HPC * DV, width), bf16),
            pltpu.VMEM((nh, tok, ocols), f32),
            pltpu.VMEM((HPC, n // 2, tok, kc), f32),
            pltpu.VMEM((HPC, tok, 128), f32),
            pltpu.VMEM((HPC, tok, 256), bf16),
            pltpu.VMEM((HPC, n // 2, kc, DV), bf16),
            pltpu.VMEM((HPC, tok, 256), f32),
            pltpu.VMEM((n // 2, tok, kc), f32),
            pltpu.VMEM((tok, HPC * DV), bf16),
            pltpu.VMEM((nchip, tok, ocols), bf16),
            pltpu.VMEM((nchip, tok, ocols), bf16),
            pltpu.VMEM((nchip - 1, tok, ocols), bf16),
            pltpu.VMEM((nchip - 1, tok, ocols), bf16),
            dma((nchunk, half)), dma((nchunk, half)), dma((nchunk, half)), dma((nchunk, half)),
            dma((half,)), dma((half,)), dma((half,)), dma((half,)),
            dma((2 * half, PARTS - 1)), dma((2 * half, PARTS - 1)),
            dma((2,)), dma((nchip,)), dma((nchip,)), dma((nchip - 1,)), dma((nchip - 1,)),
        ],
        compiler_params=pltpu.CompilerParams(
            collective_id=0, has_side_effects=True, vmem_limit_bytes=60 * 1024 * 1024
        ),
    )(block_mask, query_heads, latent, up_weight, out_weight)


def solution(mesh):
    n, nh = mesh.shape["blk"], mesh.shape["head"]
    return jax.shard_map(
        functools.partial(per_device, n, nh),
        mesh=mesh,
        in_specs=(
            P("blk", "head"), P("blk", None), P("blk", None),
            P("blk", "head"), P("head", None), P(),
        ),
        out_specs=P("blk", "head"),
        check_vma=False,
    )
```

```python
import functools
import math

import jax
import jax.numpy as jnp
from jax import lax
from jax.experimental import pallas as pl
from jax.experimental.pallas import tpu as pltpu
from jax.sharding import PartitionSpec as P

DN = 128
DR = 64
DV = 128
QB = 96
NEG = -1e30
HPC = 2
PARTS = 4
MESH = pl.DeviceIdType.MESH


def ring_place(index, n):
    return jnp.where(index % 2 == 0, index // 2, n - 1 - index // 2)


def ring_index(place, n):
    place = lax.rem(place + 2 * n, n)
    return jnp.where(place < n // 2, 2 * place, 2 * (n - 1 - place) + 1)


def kernel(
    n, nh, mask_ref, q_hbm, lat_ref, rope_ref, up_ref, ow_ref, out_ref,
    q_ref,
    wfull, lat, wo, acc, scores, peak, qs, vals, mix, bias, heads_out,
    give1, take1, give2, take2,
    cw_send, cw_recv, cc_send, cc_recv,
    lcw_send, lcw_recv, lcc_send, lcc_recv, lp_send, lp_recv,
    wo_sem, q_sem, r1_send, r1_recv, r2_send, r2_recv,
):
    tok = q_ref.shape[0]
    rows = up_ref.shape[0]
    nchunk, _, cw = wfull.shape
    half = n // 2
    kc = 2 * tok
    kvr = n * rows
    ocols = out_ref.shape[1]
    nchip = nh // 2
    my = lax.axis_index("blk")
    hd = lax.axis_index("head")
    place = ring_place(my, n)
    right = ring_index(place + 1, n)
    left = ring_index(place + n - 1, n)
    part = lax.rem(hd, PARTS)
    base = hd - part
    prow = tok // PARTS
    core = lax.rem(hd, 2)
    chip = hd // 2
    mate = chip * 2 + 1 - core
    scale = math.log2(math.e) / math.sqrt(DN + DR)

    barrier = pltpu.get_barrier_semaphore()
    for other in (left, right):
        pl.semaphore_signal(barrier, inc=1, device_id=(other, hd), device_id_type=MESH)
    for d in range(1, nh):
        pl.semaphore_signal(barrier, inc=1, device_id=(my, lax.rem(hd + d, nh)), device_id_type=MESH)
    pl.semaphore_wait(barrier, 2 + nh - 1)

    def wmsg(c, k, clockwise):
        origin = ring_index(place - (k - 1), n) if clockwise else ring_index(place + (k - 1), n)
        start, size = origin * rows, rows
        if k == half:
            size = rows // 2
            if not clockwise:
                start = start + size
        block = wfull.at[c, pl.ds(pl.multiple_of(start, 16), size), :]
        return pltpu.make_async_remote_copy(
            src_ref=block, dst_ref=block,
            send_sem=(cw_send if clockwise else cc_send).at[c, k - 1],
            recv_sem=(cw_recv if clockwise else cc_recv).at[c, k - 1],
            device_id=(right if clockwise else left, hd), device_id_type=MESH,
        )

    def wgot(c, k, clockwise):
        origin = ring_index(place - k, n) if clockwise else ring_index(place + k, n)
        start, size = origin * rows, rows
        if k == half:
            size = rows // 2
            if not clockwise:
                start = start + size
        block = wfull.at[c, pl.ds(pl.multiple_of(start, 16), size), :]
        return pltpu.make_async_remote_copy(
            src_ref=block, dst_ref=block,
            send_sem=(cw_send if clockwise else cc_send).at[c, k - 1],
            recv_sem=(cw_recv if clockwise else cc_recv).at[c, k - 1],
            device_id=(right if clockwise else left, hd), device_id_type=MESH,
        )

    def lmsg(k, clockwise, received):
        steps = k if received else k - 1
        origin = ring_index(place - steps, n) if clockwise else ring_index(place + steps, n)
        block = lat.at[origin, part]
        return pltpu.make_async_remote_copy(
            src_ref=block, dst_ref=block,
            send_sem=(lcw_send if clockwise else lcc_send).at[k - 1],
            recv_sem=(lcw_recv if clockwise else lcc_recv).at[k - 1],
            device_id=(right if clockwise else left, hd), device_id_type=MESH,
        )

    def lpeer(k, clockwise, d, received):
        origin = ring_index(place - k, n) if clockwise else ring_index(place + k, n)
        e = (k - 1) * 2 + (0 if clockwise else 1)
        owner = lax.rem(part + PARTS - d, PARTS) if received else part
        block = lat.at[origin, owner]
        return pltpu.make_async_remote_copy(
            src_ref=block, dst_ref=block,
            send_sem=lp_send.at[e, d - 1], recv_sem=lp_recv.at[e, d - 1],
            device_id=(my, base + lax.rem(part + d, PARTS)), device_id_type=MESH,
        )

    lat_hops = [(k, way) for k in range(1, half + 1) for way in (True, False) if way or k < half]

    joined = jnp.concatenate(
        [lat_ref[...], rope_ref[...], jnp.zeros((tok, 128 - DR), lat_ref.dtype)], axis=1
    )
    lat[my] = joined.reshape(PARTS, prow, kvr + 128)
    lmsg(1, True, False).start()
    lmsg(1, False, False).start()

    own_rows = pl.ds(pl.multiple_of(my * rows, 16), rows)

    def fill(c, _):
        wfull[c, own_rows, :] = up_ref[:, pl.ds(pl.multiple_of(c * cw, 128), cw)]
        return 0

    fill(0, 0)
    wmsg(0, 1, True).start()
    wmsg(0, 1, False).start()
    lax.fori_loop(1, nchunk, fill, 0)
    q_copy = pltpu.make_async_copy(q_hbm, q_ref, q_sem)
    q_copy.start()

    def wo_copy(c):
        slot = lax.rem(c, 2)
        return pltpu.make_async_copy(
            ow_ref.at[pl.ds(pl.multiple_of(c * (HPC * DV), 128), HPC * DV), :],
            wo.at[slot], wo_sem.at[slot],
        )

    nj = my // 2 + 1

    def send_group(t, k):
        c = t - (k - 1)

        @pl.when((c >= 0) & (c < nchunk))
        def _():
            if k > 1:
                wgot(c, k - 1, True).wait_recv()
            wmsg(c, k, True).start()
            if k > 1:
                wgot(c, k - 1, False).wait_recv()
            wmsg(c, k, False).start()

    def project(c, o):
        slot = lax.rem(c, 2)
        columns = pl.ds(pl.multiple_of(o * ocols, 128), ocols)
        return acc[o] + jnp.dot(
            heads_out[...], wo[slot, :, columns], preferred_element_type=jnp.float32
        )

    def phase_a(c):
        qc = q_ref[:, pl.ds(pl.multiple_of(c * (HPC * (DN + DR)), 128), HPC * (DN + DR))]
        pad = jnp.zeros((tok, 256 - DN - DR), qc.dtype)
        for h in range(HPC):
            qs[h] = jnp.concatenate([qc[:, h * (DN + DR) : (h + 1) * (DN + DR)], pad], axis=1)
            peak[h] = jnp.full((tok, 128), NEG, jnp.float32)
            mix[h] = jnp.zeros((tok, 256), jnp.float32)

        def step(j, _):
            block = lat[pl.ds(2 * j, 2)].reshape(kc, kvr + 128)
            rope = block[:, kvr:]
            kv = jnp.dot(
                block[:, :kvr], wfull[c], preferred_element_type=jnp.float32
            ).astype(jnp.bfloat16)
            for h in range(HPC):
                key = jnp.concatenate([kv[:, h * 256 : h * 256 + DN], rope], axis=1)
                vals[h, j] = kv[:, h * 256 + DN : (h + 1) * 256]
                s = lax.dot_general(
                    qs[h], key, (((1,), (1,)), ((), ())), preferred_element_type=jnp.float32
                )
                s = s * scale + bias[j]
                scores[h, j] = s
                top = peak[h]
                for g in range(kc // 128):
                    top = jnp.maximum(top, s[:, g * 128 : (g + 1) * 128])
                peak[h] = top
            return 0

        lax.fori_loop(0, nj, step, 0)

    def phase_b():
        for h in range(HPC):
            peak[h] = jnp.broadcast_to(jnp.max(peak[h], axis=1, keepdims=True), (tok, 128))
        ones = jnp.ones((kc, 128), jnp.bfloat16)

        def step(j, _):
            for h in range(HPC):
                top = peak[h]
                p = jnp.concatenate(
                    [
                        jnp.exp2(scores[h, j, :, g * 128 : (g + 1) * 128] - top).astype(jnp.bfloat16)
                        for g in range(kc // 128)
                    ],
                    axis=1,
                )
                v = jnp.concatenate([vals[h, j], ones], axis=1)
                mix[h] += jnp.dot(p, v, preferred_element_type=jnp.float32)
            return 0

        lax.fori_loop(0, nj, step, 0)
        for h in range(HPC):
            m = mix[h]
            heads_out[:, h * DV : (h + 1) * DV] = (m[:, :DV] / m[:, DV:]).astype(jnp.bfloat16)

    def tick(t, _):
        c = t - half
        live = c >= 0
        upper = list(range(half, 0, -1))
        first = upper[: max(1, half // 2)]
        second = upper[max(1, half // 2) :]
        for k in first:
            send_group(t, k)

        for k, way in lat_hops:
            @pl.when(t == k)
            def _(k=k, way=way):
                lmsg(k, way, True).wait_recv()
                if (k + 1, way) in lat_hops:
                    lmsg(k + 1, way, False).start()
                for d in range(1, PARTS):
                    lpeer(k, way, d, False).start()

        @pl.when(t == 0)
        def _():
            wo_copy(0).start()
            wo_copy(1).start()
            acc[...] = jnp.zeros_like(acc)
            lane = lax.broadcasted_iota(jnp.int32, (QB, kc), 1)
            row = lax.broadcasted_iota(jnp.int32, (QB, kc), 0)
            group = lane // QB
            for j in range(n // 2):
                for g in range(tok // QB):
                    bits = jnp.zeros((QB, kc), jnp.int32)
                    for b in range(kc // QB):
                        bit = mask_ref[my * (tok // QB) + g, j * (kc // QB) + b]
                        bits = jnp.where(group == b, bit, bits)
                    allowed = (bits == 1) & (lane + j * kc <= row + (my * tok + g * QB))
                    bias[j, g * QB : (g + 1) * QB, :] = jnp.where(allowed, 0.0, NEG)

        @pl.when(t == half)
        def _():
            q_copy.wait()
            for k, way in lat_hops:
                for d in range(1, PARTS):
                    lpeer(k, way, d, True).wait_recv()

        @pl.when(live)
        def _():
            wgot(c, half, True).wait_recv()
            wgot(c, half, False).wait_recv()
            phase_a(c)

        for k in second:
            send_group(t + 1, k)

        @pl.when(live)
        def _():
            phase_b()
            wo_copy(c).wait()

        @pl.when(live & (c < nchunk - 1))
        def _():
            def one(o, _):
                acc[o] = project(c, o)
                return 0

            lax.fori_loop(0, nh, one, 0)

            @pl.when(c + 2 < nchunk)
            def _():
                wo_copy(c + 2).start()

        return 0

    lax.fori_loop(0, nchunk + half, tick, 0)

    last = nchunk - 1

    def stage1(i):
        return pltpu.make_async_remote_copy(
            src_ref=give1.at[i], dst_ref=take1.at[i], send_sem=r1_send.at[i],
            recv_sem=r1_recv.at[i], device_id=(my, mate), device_id_type=MESH,
        )

    def stage2(i):
        to = lax.rem(chip + i, nchip) * 2 + core
        return pltpu.make_async_remote_copy(
            src_ref=give2.at[i - 1], dst_ref=take2.at[i - 1], send_sem=r2_send.at[i - 1],
            recv_sem=r2_recv.at[i - 1], device_id=(my, to), device_id_type=MESH,
        )

    order = list(range(1, nchip)) + [0]
    for i in order:
        to = lax.rem(chip + i, nchip) * 2 + 1 - core
        give1[i] = project(last, to).astype(jnp.bfloat16)
        stage1(i).start()
    for i in order[:-1]:
        to = lax.rem(chip + i, nchip) * 2 + core
        mine = project(last, to)
        stage1(i).wait_recv()
        give2[i - 1] = (mine + take1[i].astype(jnp.float32)).astype(jnp.bfloat16)
        stage2(i).start()
    total = project(last, hd)
    stage1(0).wait_recv()
    total = total + take1[0].astype(jnp.float32)
    acc[0] = total
    for i in order[:-1]:
        stage2(i).wait_recv()
        acc[0] += take2[i - 1].astype(jnp.float32)
    out_ref[...] = acc[0].astype(jnp.bfloat16)

    def drain(c, _):
        for k in range(1, half + 1):
            wmsg(c, k, True).wait_send()
            wmsg(c, k, False).wait_send()
        return 0

    lax.fori_loop(0, nchunk, drain, 0)
    for k, way in lat_hops:
        lmsg(k, way, False).wait_send()
        for d in range(1, PARTS):
            lpeer(k, way, d, False).wait_send()
    for i in order:
        stage1(i).wait_send()
    for i in order[:-1]:
        stage2(i).wait_send()


def per_device(n, nh, query_heads, latent_cache, rope_keys, up_weight, out_weight, block_mask):
    tok = query_heads.shape[0]
    heads = out_weight.shape[0] // DV
    kvr = latent_cache.shape[1]
    rows = up_weight.shape[0]
    width = out_weight.shape[1]
    ocols = width // nh
    nchunk = heads // HPC
    half = n // 2
    kc = 2 * tok
    lw = kvr + 128
    bf16, f32 = jnp.bfloat16, jnp.float32
    dma = pltpu.SemaphoreType.DMA
    nchip = nh // 2
    vmem = pl.BlockSpec(memory_space=pltpu.VMEM)
    return pl.pallas_call(
        functools.partial(kernel, n, nh),
        out_shape=jax.ShapeDtypeStruct((tok, ocols), bf16),
        in_specs=[
            pl.BlockSpec(memory_space=pltpu.SMEM), pl.BlockSpec(memory_space=pl.ANY),
            vmem, vmem, vmem, pl.BlockSpec(memory_space=pl.ANY),
        ],
        out_specs=vmem,
        scratch_shapes=[
            pltpu.VMEM(query_heads.shape, bf16),
            pltpu.VMEM((nchunk, kvr, HPC * 256), bf16),
            pltpu.VMEM((n, PARTS, tok // PARTS, lw), bf16),
            pltpu.VMEM((2, HPC * DV, width), bf16),
            pltpu.VMEM((nh, tok, ocols), f32),
            pltpu.VMEM((HPC, n // 2, tok, kc), f32),
            pltpu.VMEM((HPC, tok, 128), f32),
            pltpu.VMEM((HPC, tok, 256), bf16),
            pltpu.VMEM((HPC, n // 2, kc, DV), bf16),
            pltpu.VMEM((HPC, tok, 256), f32),
            pltpu.VMEM((n // 2, tok, kc), f32),
            pltpu.VMEM((tok, HPC * DV), bf16),
            pltpu.VMEM((nchip, tok, ocols), bf16),
            pltpu.VMEM((nchip, tok, ocols), bf16),
            pltpu.VMEM((nchip - 1, tok, ocols), bf16),
            pltpu.VMEM((nchip - 1, tok, ocols), bf16),
            dma((nchunk, half)), dma((nchunk, half)), dma((nchunk, half)), dma((nchunk, half)),
            dma((half,)), dma((half,)), dma((half,)), dma((half,)),
            dma((2 * half, PARTS - 1)), dma((2 * half, PARTS - 1)),
            dma((2,)), dma, dma((nchip,)), dma((nchip,)), dma((nchip - 1,)), dma((nchip - 1,)),
        ],
        compiler_params=pltpu.CompilerParams(
            collective_id=0, has_side_effects=True, vmem_limit_bytes=60 * 1024 * 1024
        ),
    )(block_mask, query_heads, latent_cache, rope_keys, up_weight, out_weight)


def solution(mesh):
    n, nh = mesh.shape["blk"], mesh.shape["head"]
    return jax.shard_map(
        functools.partial(per_device, n, nh),
        mesh=mesh,
        in_specs=(
            P("blk", "head"), P("blk", None), P("blk", None),
            P("blk", "head"), P("head", None), P(),
        ),
        out_specs=P("blk", "head"),
        check_vma=False,
    )
```

```python
import functools
import math

import jax
import jax.numpy as jnp
from jax import lax
from jax.experimental import pallas as pl
from jax.experimental.pallas import tpu as pltpu
from jax.sharding import PartitionSpec as P

DN = 128
DR = 64
DV = 128
QB = 96
NEG = -1e30
HPC = 4
HPM = 2
SUB = HPC // HPM
PARTS = 4
MESH = pl.DeviceIdType.MESH


def ring_place(index, n):
    return jnp.where(index % 2 == 0, index // 2, n - 1 - index // 2)


def ring_index(place, n):
    place = lax.rem(place + 2 * n, n)
    return jnp.where(place < n // 2, 2 * place, 2 * (n - 1 - place) + 1)


def kernel(
    n, nh, mask_ref, q_hbm, lat_ref, rope_ref, up_ref, ow_ref, out_ref,
    q_ref,
    wfull, lat, wo, acc, scores, peak, qs, vals, mix, bias, heads_out,
    give1, take1, give2, take2,
    cw_send, cw_recv, cc_send, cc_recv,
    lcw_send, lcw_recv, lcc_send, lcc_recv, lp_send, lp_recv,
    wo_sem, q_sem, r1_send, r1_recv, r2_send, r2_recv,
):
    tok = q_ref.shape[0]
    rows = up_ref.shape[0]
    nsub, _, cw = wfull.shape
    nchunk = nsub // SUB
    half = n // 2
    kc = 2 * tok
    kvr = n * rows
    ocols = out_ref.shape[1]
    nchip = nh // 2
    my = lax.axis_index("blk")
    hd = lax.axis_index("head")
    place = ring_place(my, n)
    right = ring_index(place + 1, n)
    left = ring_index(place + n - 1, n)
    part = lax.rem(hd, PARTS)
    base = hd - part
    prow = tok // PARTS
    core = lax.rem(hd, 2)
    chip = hd // 2
    mate = chip * 2 + 1 - core
    scale = math.log2(math.e) / math.sqrt(DN + DR)

    barrier = pltpu.get_barrier_semaphore()
    for other in (left, right):
        pl.semaphore_signal(barrier, inc=1, device_id=(other, hd), device_id_type=MESH)
    for d in range(1, nh):
        pl.semaphore_signal(barrier, inc=1, device_id=(my, lax.rem(hd + d, nh)), device_id_type=MESH)
    pl.semaphore_wait(barrier, 2 + nh - 1)

    def wmsg(c, k, clockwise):
        origin = ring_index(place - (k - 1), n) if clockwise else ring_index(place + (k - 1), n)
        start, size = origin * rows, rows
        if k == half:
            size = rows // 2
            if not clockwise:
                start = start + size
        block = wfull.at[c, pl.ds(pl.multiple_of(start, 16), size), :]
        return pltpu.make_async_remote_copy(
            src_ref=block, dst_ref=block,
            send_sem=(cw_send if clockwise else cc_send).at[c, k - 1],
            recv_sem=(cw_recv if clockwise else cc_recv).at[c, k - 1],
            device_id=(right if clockwise else left, hd), device_id_type=MESH,
        )

    def wgot(c, k, clockwise):
        origin = ring_index(place - k, n) if clockwise else ring_index(place + k, n)
        start, size = origin * rows, rows
        if k == half:
            size = rows // 2
            if not clockwise:
                start = start + size
        block = wfull.at[c, pl.ds(pl.multiple_of(start, 16), size), :]
        return pltpu.make_async_remote_copy(
            src_ref=block, dst_ref=block,
            send_sem=(cw_send if clockwise else cc_send).at[c, k - 1],
            recv_sem=(cw_recv if clockwise else cc_recv).at[c, k - 1],
            device_id=(right if clockwise else left, hd), device_id_type=MESH,
        )

    def lmsg(k, clockwise, received):
        steps = k if received else k - 1
        origin = ring_index(place - steps, n) if clockwise else ring_index(place + steps, n)
        block = lat.at[origin, part]
        return pltpu.make_async_remote_copy(
            src_ref=block, dst_ref=block,
            send_sem=(lcw_send if clockwise else lcc_send).at[k - 1],
            recv_sem=(lcw_recv if clockwise else lcc_recv).at[k - 1],
            device_id=(right if clockwise else left, hd), device_id_type=MESH,
        )

    def lpeer(k, clockwise, d, received):
        origin = ring_index(place - k, n) if clockwise else ring_index(place + k, n)
        e = (k - 1) * 2 + (0 if clockwise else 1)
        owner = lax.rem(part + PARTS - d, PARTS) if received else part
        block = lat.at[origin, owner]
        return pltpu.make_async_remote_copy(
            src_ref=block, dst_ref=block,
            send_sem=lp_send.at[e, d - 1], recv_sem=lp_recv.at[e, d - 1],
            device_id=(my, base + lax.rem(part + d, PARTS)), device_id_type=MESH,
        )

    lat_hops = [(k, way) for k in range(1, half + 1) for way in (True, False) if way or k < half]

    joined = jnp.concatenate(
        [lat_ref[...], rope_ref[...], jnp.zeros((tok, 128 - DR), lat_ref.dtype)], axis=1
    )
    lat[my] = joined.reshape(PARTS, prow, kvr + 128)
    lmsg(1, True, False).start()
    lmsg(1, False, False).start()

    own_rows = pl.ds(pl.multiple_of(my * rows, 16), rows)

    def fill(c, _):
        wfull[c, own_rows, :] = up_ref[:, pl.ds(pl.multiple_of(c * cw, 128), cw)]
        return 0

    fill(0, 0)
    wmsg(0, 1, True).start()
    wmsg(0, 1, False).start()
    lax.fori_loop(1, nsub, fill, 0)
    q_copy = pltpu.make_async_copy(q_hbm, q_ref, q_sem)
    q_copy.start()

    def wo_copy(c):
        slot = lax.rem(c, 2)
        return pltpu.make_async_copy(
            ow_ref.at[pl.ds(pl.multiple_of(c * (HPC * DV), 128), HPC * DV), :],
            wo.at[slot], wo_sem.at[slot],
        )

    nj = my // 2 + 1

    def send_group(t, k):
        c = t - (k - 1)

        @pl.when((c >= 0) & (c < nsub))
        def _():
            if k > 1:
                wgot(c, k - 1, True).wait_recv()
            wmsg(c, k, True).start()
            if k > 1:
                wgot(c, k - 1, False).wait_recv()
            wmsg(c, k, False).start()

    def project(c, o):
        slot = lax.rem(c, 2)
        columns = pl.ds(pl.multiple_of(o * ocols, 128), ocols)
        return acc[o] + jnp.dot(
            heads_out[...], wo[slot, :, columns], preferred_element_type=jnp.float32
        )

    def phase_a(c):
        qc = q_ref[:, pl.ds(pl.multiple_of(c * (HPC * (DN + DR)), 128), HPC * (DN + DR))]
        pad = jnp.zeros((tok, 256 - DN - DR), qc.dtype)
        for h in range(HPC):
            qs[h] = jnp.concatenate([qc[:, h * (DN + DR) : (h + 1) * (DN + DR)], pad], axis=1)
            peak[h] = jnp.full((tok, 128), NEG, jnp.float32)
            mix[h] = jnp.zeros((tok, 256), jnp.float32)

        def step(j, _):
            block = lat[pl.ds(2 * j, 2)].reshape(kc, kvr + 128)
            rope = block[:, kvr:]
            kvs = [
                jnp.dot(
                    block[:, :kvr], wfull[c * SUB + i], preferred_element_type=jnp.float32
                ).astype(jnp.bfloat16)
                for i in range(SUB)
            ]
            for h in range(HPC):
                kv, at = kvs[h // HPM], (h % HPM) * 256
                key = jnp.concatenate([kv[:, at : at + DN], rope], axis=1)
                vals[h, j] = kv[:, at + DN : at + 256]
                s = lax.dot_general(
                    qs[h], key, (((1,), (1,)), ((), ())), preferred_element_type=jnp.float32
                )
                s = s * scale + bias[j]
                scores[h, j] = s
                top = peak[h]
                for g in range(kc // 128):
                    top = jnp.maximum(top, s[:, g * 128 : (g + 1) * 128])
                peak[h] = top
            return 0

        lax.fori_loop(0, nj, step, 0)

    def phase_b():
        for h in range(HPC):
            peak[h] = jnp.broadcast_to(jnp.max(peak[h], axis=1, keepdims=True), (tok, 128))
        ones = jnp.ones((kc, 128), jnp.bfloat16)

        def step(j, _):
            for h in range(HPC):
                top = peak[h]
                p = jnp.concatenate(
                    [
                        jnp.exp2(scores[h, j, :, g * 128 : (g + 1) * 128] - top).astype(jnp.bfloat16)
                        for g in range(kc // 128)
                    ],
                    axis=1,
                )
                v = jnp.concatenate([vals[h, j], ones], axis=1)
                mix[h] += jnp.dot(p, v, preferred_element_type=jnp.float32)
            return 0

        lax.fori_loop(0, nj, step, 0)
        for h in range(HPC):
            m = mix[h]
            heads_out[:, h * DV : (h + 1) * DV] = (m[:, :DV] / m[:, DV:]).astype(jnp.bfloat16)

    def tick(t, _):
        u = t - half - 1
        c = u // SUB
        for k in range(half, 0, -1):
            send_group(t if k > half // 2 else t + 1, k)

        for k, way in lat_hops:
            @pl.when(t == k)
            def _(k=k, way=way):
                lmsg(k, way, True).wait_recv()
                if (k + 1, way) in lat_hops:
                    lmsg(k + 1, way, False).start()
                for d in range(1, PARTS):
                    lpeer(k, way, d, False).start()

        @pl.when(t == 0)
        def _():
            wo_copy(0).start()
            wo_copy(1).start()
            acc[...] = jnp.zeros_like(acc)
            lane = lax.broadcasted_iota(jnp.int32, (QB, kc), 1)
            row = lax.broadcasted_iota(jnp.int32, (QB, kc), 0)
            group = lane // QB
            for j in range(n // 2):
                for g in range(tok // QB):
                    bits = jnp.zeros((QB, kc), jnp.int32)
                    for b in range(kc // QB):
                        bit = mask_ref[my * (tok // QB) + g, j * (kc // QB) + b]
                        bits = jnp.where(group == b, bit, bits)
                    allowed = (bits == 1) & (lane + j * kc <= row + (my * tok + g * QB))
                    bias[j, g * QB : (g + 1) * QB, :] = jnp.where(allowed, 0.0, NEG)

        @pl.when(t == half + 1)
        def _():
            q_copy.wait()
            for k, way in lat_hops:
                for d in range(1, PARTS):
                    lpeer(k, way, d, True).wait_recv()

        @pl.when((u >= 0) & (lax.rem(u, SUB) == 0))
        def _():
            for i in range(SUB):
                wgot(c * SUB + i, half, True).wait_recv()
                wgot(c * SUB + i, half, False).wait_recv()
            phase_a(c)

        done = (u >= 0) & (lax.rem(u, SUB) == SUB - 1)

        @pl.when(done)
        def _():
            phase_b()
            wo_copy(c).wait()

        @pl.when(done & (c < nchunk - 1))
        def _():
            def one(o, _):
                acc[o] = project(c, o)
                return 0

            lax.fori_loop(0, nh, one, 0)

            @pl.when(c + 2 < nchunk)
            def _():
                wo_copy(c + 2).start()

        return 0

    lax.fori_loop(0, nsub + half + 1, tick, 0)

    last = nchunk - 1

    def stage1(i):
        return pltpu.make_async_remote_copy(
            src_ref=give1.at[i], dst_ref=take1.at[i], send_sem=r1_send.at[i],
            recv_sem=r1_recv.at[i], device_id=(my, mate), device_id_type=MESH,
        )

    def stage2(i):
        to = lax.rem(chip + i, nchip) * 2 + core
        return pltpu.make_async_remote_copy(
            src_ref=give2.at[i - 1], dst_ref=take2.at[i - 1], send_sem=r2_send.at[i - 1],
            recv_sem=r2_recv.at[i - 1], device_id=(my, to), device_id_type=MESH,
        )

    order = list(range(1, nchip)) + [0]
    for i in order:
        to = lax.rem(chip + i, nchip) * 2 + 1 - core
        give1[i] = project(last, to).astype(jnp.bfloat16)
        stage1(i).start()
    for i in order[:-1]:
        to = lax.rem(chip + i, nchip) * 2 + core
        mine = project(last, to)
        stage1(i).wait_recv()
        give2[i - 1] = (mine + take1[i].astype(jnp.float32)).astype(jnp.bfloat16)
        stage2(i).start()
    total = project(last, hd)
    stage1(0).wait_recv()
    total = total + take1[0].astype(jnp.float32)
    acc[0] = total
    for i in order[:-1]:
        stage2(i).wait_recv()
        acc[0] += take2[i - 1].astype(jnp.float32)
    out_ref[...] = acc[0].astype(jnp.bfloat16)

    def drain(c, _):
        for k in range(1, half + 1):
            wmsg(c, k, True).wait_send()
            wmsg(c, k, False).wait_send()
        return 0

    lax.fori_loop(0, nsub, drain, 0)
    for k, way in lat_hops:
        lmsg(k, way, False).wait_send()
        for d in range(1, PARTS):
            lpeer(k, way, d, False).wait_send()
    for i in order:
        stage1(i).wait_send()
    for i in order[:-1]:
        stage2(i).wait_send()


def per_device(n, nh, query_heads, latent_cache, rope_keys, up_weight, out_weight, block_mask):
    tok = query_heads.shape[0]
    heads = out_weight.shape[0] // DV
    kvr = latent_cache.shape[1]
    rows = up_weight.shape[0]
    width = out_weight.shape[1]
    ocols = width // nh
    nsub = heads // HPM
    half = n // 2
    kc = 2 * tok
    lw = kvr + 128
    bf16, f32 = jnp.bfloat16, jnp.float32
    dma = pltpu.SemaphoreType.DMA
    nchip = nh // 2
    vmem = pl.BlockSpec(memory_space=pltpu.VMEM)
    return pl.pallas_call(
        functools.partial(kernel, n, nh),
        out_shape=jax.ShapeDtypeStruct((tok, ocols), bf16),
        in_specs=[
            pl.BlockSpec(memory_space=pltpu.SMEM), pl.BlockSpec(memory_space=pl.ANY),
            vmem, vmem, vmem, pl.BlockSpec(memory_space=pl.ANY),
        ],
        out_specs=vmem,
        scratch_shapes=[
            pltpu.VMEM(query_heads.shape, bf16),
            pltpu.VMEM((nsub, kvr, HPM * 256), bf16),
            pltpu.VMEM((n, PARTS, tok // PARTS, lw), bf16),
            pltpu.VMEM((2, HPC * DV, width), bf16),
            pltpu.VMEM((nh, tok, ocols), f32),
            pltpu.VMEM((HPC, n // 2, tok, kc), f32),
            pltpu.VMEM((HPC, tok, 128), f32),
            pltpu.VMEM((HPC, tok, 256), bf16),
            pltpu.VMEM((HPC, n // 2, kc, DV), bf16),
            pltpu.VMEM((HPC, tok, 256), f32),
            pltpu.VMEM((n // 2, tok, kc), f32),
            pltpu.VMEM((tok, HPC * DV), bf16),
            pltpu.VMEM((nchip, tok, ocols), bf16),
            pltpu.VMEM((nchip, tok, ocols), bf16),
            pltpu.VMEM((nchip - 1, tok, ocols), bf16),
            pltpu.VMEM((nchip - 1, tok, ocols), bf16),
            dma((nsub, half)), dma((nsub, half)), dma((nsub, half)), dma((nsub, half)),
            dma((half,)), dma((half,)), dma((half,)), dma((half,)),
            dma((2 * half, PARTS - 1)), dma((2 * half, PARTS - 1)),
            dma((2,)), dma, dma((nchip,)), dma((nchip,)), dma((nchip - 1,)), dma((nchip - 1,)),
        ],
        compiler_params=pltpu.CompilerParams(
            collective_id=0, has_side_effects=True, vmem_limit_bytes=60 * 1024 * 1024
        ),
    )(block_mask, query_heads, latent_cache, rope_keys, up_weight, out_weight)


def solution(mesh):
    n, nh = mesh.shape["blk"], mesh.shape["head"]
    return jax.shard_map(
        functools.partial(per_device, n, nh),
        mesh=mesh,
        in_specs=(
            P("blk", "head"), P("blk", None), P("blk", None),
            P("blk", "head"), P("head", None), P(),
        ),
        out_specs=P("blk", "head"),
        check_vma=False,
    )
```

```python
import functools
import math

import jax
import jax.numpy as jnp
from jax import lax
from jax.experimental import pallas as pl
from jax.experimental.pallas import tpu as pltpu
from jax.sharding import PartitionSpec as P

DN = 128
DR = 64
DV = 128
QB = 96
NEG = -1e30
HPC = 4
PARTS = 4
MESH = pl.DeviceIdType.MESH


def ring_place(index, n):
    return jnp.where(index % 2 == 0, index // 2, n - 1 - index // 2)


def ring_index(place, n):
    place = lax.rem(place + 2 * n, n)
    return jnp.where(place < n // 2, 2 * place, 2 * (n - 1 - place) + 1)


def kernel(
    n, nh, mask_ref, q_hbm, lat_ref, rope_ref, up_ref, ow_ref, out_ref,
    q_ref,
    wfull, lat, wo, acc, scores, peak, qs, vals, mix, bias, heads_out,
    give1, take1, give2, take2,
    cw_send, cw_recv, cc_send, cc_recv,
    lcw_send, lcw_recv, lcc_send, lcc_recv, lp_send, lp_recv,
    wo_sem, q_sem, r1_send, r1_recv, r2_send, r2_recv,
):
    tok = q_ref.shape[0]
    rows = up_ref.shape[0]
    nchunk, _, cw = wfull.shape
    half = n // 2
    kc = 2 * tok
    kvr = n * rows
    ocols = out_ref.shape[1]
    nchip = nh // 2
    my = lax.axis_index("blk")
    hd = lax.axis_index("head")
    place = ring_place(my, n)
    right = ring_index(place + 1, n)
    left = ring_index(place + n - 1, n)
    part = lax.rem(hd, PARTS)
    base = hd - part
    prow = tok // PARTS
    core = lax.rem(hd, 2)
    chip = hd // 2
    mate = chip * 2 + 1 - core
    scale = math.log2(math.e) / math.sqrt(DN + DR)

    barrier = pltpu.get_barrier_semaphore()
    for other in (left, right):
        pl.semaphore_signal(barrier, inc=1, device_id=(other, hd), device_id_type=MESH)
    for d in range(1, nh):
        pl.semaphore_signal(barrier, inc=1, device_id=(my, lax.rem(hd + d, nh)), device_id_type=MESH)
    pl.semaphore_wait(barrier, 2 + nh - 1)

    def wmsg(c, k, clockwise):
        origin = ring_index(place - (k - 1), n) if clockwise else ring_index(place + (k - 1), n)
        start, size = origin * rows, rows
        if k == half:
            size = rows // 2
            if not clockwise:
                start = start + size
        block = wfull.at[c, pl.ds(pl.multiple_of(start, 16), size), :]
        return pltpu.make_async_remote_copy(
            src_ref=block, dst_ref=block,
            send_sem=(cw_send if clockwise else cc_send).at[c, k - 1],
            recv_sem=(cw_recv if clockwise else cc_recv).at[c, k - 1],
            device_id=(right if clockwise else left, hd), device_id_type=MESH,
        )

    def wgot(c, k, clockwise):
        origin = ring_index(place - k, n) if clockwise else ring_index(place + k, n)
        start, size = origin * rows, rows
        if k == half:
            size = rows // 2
            if not clockwise:
                start = start + size
        block = wfull.at[c, pl.ds(pl.multiple_of(start, 16), size), :]
        return pltpu.make_async_remote_copy(
            src_ref=block, dst_ref=block,
            send_sem=(cw_send if clockwise else cc_send).at[c, k - 1],
            recv_sem=(cw_recv if clockwise else cc_recv).at[c, k - 1],
            device_id=(right if clockwise else left, hd), device_id_type=MESH,
        )

    def lmsg(k, clockwise, received):
        steps = k if received else k - 1
        origin = ring_index(place - steps, n) if clockwise else ring_index(place + steps, n)
        block = lat.at[origin, part]
        return pltpu.make_async_remote_copy(
            src_ref=block, dst_ref=block,
            send_sem=(lcw_send if clockwise else lcc_send).at[k - 1],
            recv_sem=(lcw_recv if clockwise else lcc_recv).at[k - 1],
            device_id=(right if clockwise else left, hd), device_id_type=MESH,
        )

    def lpeer(k, clockwise, d, received):
        origin = ring_index(place - k, n) if clockwise else ring_index(place + k, n)
        e = (k - 1) * 2 + (0 if clockwise else 1)
        owner = lax.rem(part + PARTS - d, PARTS) if received else part
        block = lat.at[origin, owner]
        return pltpu.make_async_remote_copy(
            src_ref=block, dst_ref=block,
            send_sem=lp_send.at[e, d - 1], recv_sem=lp_recv.at[e, d - 1],
            device_id=(my, base + lax.rem(part + d, PARTS)), device_id_type=MESH,
        )

    lat_hops = [(k, way) for k in range(1, half + 1) for way in (True, False) if way or k < half]

    joined = jnp.concatenate(
        [lat_ref[...], rope_ref[...], jnp.zeros((tok, 128 - DR), lat_ref.dtype)], axis=1
    )
    lat[my] = joined.reshape(PARTS, prow, kvr + 128)
    lmsg(1, True, False).start()
    lmsg(1, False, False).start()

    own_rows = pl.ds(pl.multiple_of(my * rows, 16), rows)

    def fill(c, _):
        wfull[c, own_rows, :] = up_ref[:, pl.ds(pl.multiple_of(c * cw, 128), cw)]
        return 0

    lax.fori_loop(0, nchunk, fill, 0)
    q_copy = pltpu.make_async_copy(q_hbm, q_ref, q_sem)
    q_copy.start()

    def wo_copy(c):
        slot = lax.rem(c, 2)
        return pltpu.make_async_copy(
            ow_ref.at[pl.ds(pl.multiple_of(c * (HPC * DV), 128), HPC * DV), :],
            wo.at[slot], wo_sem.at[slot],
        )

    nj = my // 2 + 1

    def send_group(t, k):
        c = t - (k - 1)

        @pl.when((c >= 0) & (c < nchunk))
        def _():
            if k > 1:
                wgot(c, k - 1, True).wait_recv()
            wmsg(c, k, True).start()
            if k > 1:
                wgot(c, k - 1, False).wait_recv()
            wmsg(c, k, False).start()

    def project(c, o):
        slot = lax.rem(c, 2)
        columns = pl.ds(pl.multiple_of(o * ocols, 128), ocols)
        return acc[o] + jnp.dot(
            heads_out[...], wo[slot, :, columns], preferred_element_type=jnp.float32
        )

    def phase_a(c):
        qc = q_ref[:, pl.ds(pl.multiple_of(c * (HPC * (DN + DR)), 128), HPC * (DN + DR))]
        pad = jnp.zeros((tok, 256 - DN - DR), qc.dtype)
        for h in range(HPC):
            qs[h] = jnp.concatenate([qc[:, h * (DN + DR) : (h + 1) * (DN + DR)], pad], axis=1)
            peak[h] = jnp.full((tok, 128), NEG, jnp.float32)
            mix[h] = jnp.zeros((tok, 256), jnp.float32)

        def step(j, _):
            block = lat[pl.ds(2 * j, 2)].reshape(kc, kvr + 128)
            rope = block[:, kvr:]
            kv = jnp.dot(
                block[:, :kvr], wfull[c], preferred_element_type=jnp.float32
            ).astype(jnp.bfloat16)
            for h in range(HPC):
                key = jnp.concatenate([kv[:, h * 256 : h * 256 + DN], rope], axis=1)
                vals[h, j] = kv[:, h * 256 + DN : (h + 1) * 256]
                s = lax.dot_general(
                    qs[h], key, (((1,), (1,)), ((), ())), preferred_element_type=jnp.float32
                )
                s = s * scale + bias[j]
                scores[h, j] = s
                top = peak[h]
                for g in range(kc // 128):
                    top = jnp.maximum(top, s[:, g * 128 : (g + 1) * 128])
                peak[h] = top
            return 0

        lax.fori_loop(0, nj, step, 0)

    def phase_b():
        for h in range(HPC):
            peak[h] = jnp.broadcast_to(jnp.max(peak[h], axis=1, keepdims=True), (tok, 128))
        ones = jnp.ones((kc, 128), jnp.bfloat16)

        def step(j, _):
            for h in range(HPC):
                top = peak[h]
                p = jnp.concatenate(
                    [
                        jnp.exp2(scores[h, j, :, g * 128 : (g + 1) * 128] - top).astype(jnp.bfloat16)
                        for g in range(kc // 128)
                    ],
                    axis=1,
                )
                v = jnp.concatenate([vals[h, j], ones], axis=1)
                mix[h] += jnp.dot(p, v, preferred_element_type=jnp.float32)
            return 0

        lax.fori_loop(0, nj, step, 0)
        for h in range(HPC):
            m = mix[h]
            heads_out[:, h * DV : (h + 1) * DV] = (m[:, :DV] / m[:, DV:]).astype(jnp.bfloat16)

    def tick(t, _):
        c = t - half
        live = c >= 0
        upper = list(range(half, 0, -1))
        first = upper[: max(1, half // 2)]
        second = upper[max(1, half // 2) :]
        for k in first:
            send_group(t, k)

        for k, way in lat_hops:
            @pl.when(t == k)
            def _(k=k, way=way):
                lmsg(k, way, True).wait_recv()
                if (k + 1, way) in lat_hops:
                    lmsg(k + 1, way, False).start()
                for d in range(1, PARTS):
                    lpeer(k, way, d, False).start()

        @pl.when(t == 0)
        def _():
            wo_copy(0).start()
            wo_copy(1).start()
            acc[...] = jnp.zeros_like(acc)
            lane = lax.broadcasted_iota(jnp.int32, (QB, kc), 1)
            row = lax.broadcasted_iota(jnp.int32, (QB, kc), 0)
            group = lane // QB
            for j in range(n // 2):
                for g in range(tok // QB):
                    bits = jnp.zeros((QB, kc), jnp.int32)
                    for b in range(kc // QB):
                        bit = mask_ref[my * (tok // QB) + g, j * (kc // QB) + b]
                        bits = jnp.where(group == b, bit, bits)
                    allowed = (bits == 1) & (lane + j * kc <= row + (my * tok + g * QB))
                    bias[j, g * QB : (g + 1) * QB, :] = jnp.where(allowed, 0.0, NEG)

        @pl.when(t == half)
        def _():
            q_copy.wait()
            for k, way in lat_hops:
                for d in range(1, PARTS):
                    lpeer(k, way, d, True).wait_recv()

        @pl.when(live)
        def _():
            wgot(c, half, True).wait_recv()
            wgot(c, half, False).wait_recv()
            phase_a(c)

        for k in second:
            send_group(t, k)

        @pl.when(live)
        def _():
            phase_b()
            wo_copy(c).wait()

        @pl.when(live & (c < nchunk - 1))
        def _():
            def one(o, _):
                acc[o] = project(c, o)
                return 0

            lax.fori_loop(0, nh, one, 0)

            @pl.when(c + 2 < nchunk)
            def _():
                wo_copy(c + 2).start()

        return 0

    lax.fori_loop(0, nchunk + half, tick, 0)

    last = nchunk - 1

    def stage1(i):
        return pltpu.make_async_remote_copy(
            src_ref=give1.at[i], dst_ref=take1.at[i], send_sem=r1_send.at[i],
            recv_sem=r1_recv.at[i], device_id=(my, mate), device_id_type=MESH,
        )

    def stage2(i):
        to = lax.rem(chip + i, nchip) * 2 + core
        return pltpu.make_async_remote_copy(
            src_ref=give2.at[i - 1], dst_ref=take2.at[i - 1], send_sem=r2_send.at[i - 1],
            recv_sem=r2_recv.at[i - 1], device_id=(my, to), device_id_type=MESH,
        )

    order = list(range(1, nchip)) + [0]
    for i in order:
        to = lax.rem(chip + i, nchip) * 2 + 1 - core
        give1[i] = project(last, to).astype(jnp.bfloat16)
        stage1(i).start()
    for i in order[:-1]:
        to = lax.rem(chip + i, nchip) * 2 + core
        mine = project(last, to)
        stage1(i).wait_recv()
        give2[i - 1] = (mine + take1[i].astype(jnp.float32)).astype(jnp.bfloat16)
        stage2(i).start()
    total = project(last, hd)
    stage1(0).wait_recv()
    total = total + take1[0].astype(jnp.float32)
    acc[0] = total
    for i in order[:-1]:
        stage2(i).wait_recv()
        acc[0] += take2[i - 1].astype(jnp.float32)
    out_ref[...] = acc[0].astype(jnp.bfloat16)

    def drain(c, _):
        for k in range(1, half + 1):
            wmsg(c, k, True).wait_send()
            wmsg(c, k, False).wait_send()
        return 0

    lax.fori_loop(0, nchunk, drain, 0)
    for k, way in lat_hops:
        lmsg(k, way, False).wait_send()
        for d in range(1, PARTS):
            lpeer(k, way, d, False).wait_send()
    for i in order:
        stage1(i).wait_send()
    for i in order[:-1]:
        stage2(i).wait_send()


def per_device(n, nh, query_heads, latent_cache, rope_keys, up_weight, out_weight, block_mask):
    tok = query_heads.shape[0]
    heads = out_weight.shape[0] // DV
    kvr = latent_cache.shape[1]
    rows = up_weight.shape[0]
    width = out_weight.shape[1]
    ocols = width // nh
    nchunk = heads // HPC
    half = n // 2
    kc = 2 * tok
    lw = kvr + 128
    bf16, f32 = jnp.bfloat16, jnp.float32
    dma = pltpu.SemaphoreType.DMA
    nchip = nh // 2
    vmem = pl.BlockSpec(memory_space=pltpu.VMEM)
    return pl.pallas_call(
        functools.partial(kernel, n, nh),
        out_shape=jax.ShapeDtypeStruct((tok, ocols), bf16),
        in_specs=[
            pl.BlockSpec(memory_space=pltpu.SMEM), pl.BlockSpec(memory_space=pl.ANY),
            vmem, vmem, vmem, pl.BlockSpec(memory_space=pl.ANY),
        ],
        out_specs=vmem,
        scratch_shapes=[
            pltpu.VMEM(query_heads.shape, bf16),
            pltpu.VMEM((nchunk, kvr, HPC * 256), bf16),
            pltpu.VMEM((n, PARTS, tok // PARTS, lw), bf16),
            pltpu.VMEM((2, HPC * DV, width), bf16),
            pltpu.VMEM((nh, tok, ocols), f32),
            pltpu.VMEM((HPC, n // 2, tok, kc), f32),
            pltpu.VMEM((HPC, tok, 128), f32),
            pltpu.VMEM((HPC, tok, 256), bf16),
            pltpu.VMEM((HPC, n // 2, kc, DV), bf16),
            pltpu.VMEM((HPC, tok, 256), f32),
            pltpu.VMEM((n // 2, tok, kc), f32),
            pltpu.VMEM((tok, HPC * DV), bf16),
            pltpu.VMEM((nchip, tok, ocols), bf16),
            pltpu.VMEM((nchip, tok, ocols), bf16),
            pltpu.VMEM((nchip - 1, tok, ocols), bf16),
            pltpu.VMEM((nchip - 1, tok, ocols), bf16),
            dma((nchunk, half)), dma((nchunk, half)), dma((nchunk, half)), dma((nchunk, half)),
            dma((half,)), dma((half,)), dma((half,)), dma((half,)),
            dma((2 * half, PARTS - 1)), dma((2 * half, PARTS - 1)),
            dma((2,)), dma, dma((nchip,)), dma((nchip,)), dma((nchip - 1,)), dma((nchip - 1,)),
        ],
        compiler_params=pltpu.CompilerParams(
            collective_id=0, has_side_effects=True, vmem_limit_bytes=60 * 1024 * 1024
        ),
    )(block_mask, query_heads, latent_cache, rope_keys, up_weight, out_weight)


def solution(mesh):
    n, nh = mesh.shape["blk"], mesh.shape["head"]
    return jax.shard_map(
        functools.partial(per_device, n, nh),
        mesh=mesh,
        in_specs=(
            P("blk", "head"), P("blk", None), P("blk", None),
            P("blk", "head"), P("head", None), P(),
        ),
        out_specs=P("blk", "head"),
        check_vma=False,
    )
```
